1024 devices in a mesh: replica: 16 (over x, z_hi), fsdp: 8 (over z_lo), tensor: 8 (over y, core).
Axes of the slice: x: 4, y: 4, z: 32 (z_hi: 4, z_lo: 8; z = z_hi * 8 + z_lo), core: 2. Of those that a mesh axis runs over, the one named last changes fastest.
Arguments:
- master: float32 [8192, 8, 2048], P(('fsdp', 'tensor'), None, 'replica'), may hold values from -6 to 6
- gradient: bfloat16 [8192, 8, 2048], P(('fsdp', 'tensor'), None, 'replica'), may hold values from -6 to 6
- first_moment: float32 [8192, 8, 2048], P(('fsdp', 'tensor'), None, 'replica'), may hold values from -3 to 3
- second_moment: float32 [8192, 8, 2048], P(('fsdp', 'tensor'), None, 'replica'), may hold values from 0.1 to 4
Outputs:
- new_master: float32 [8192, 8, 2048], P(('fsdp', 'tensor'), None, 'replica')
- rollout: bfloat16 [8192, 8, 2048], P('fsdp', 'tensor')
The draws below stay inside these ranges and needn't reach their ends.
All inputs are finite; a program needn't handle non-finite values.
Results may differ from the reference program's by a relative error of at most 0.001.
Values may be sent and summed in bfloat16 or wider, within the bound.
No kernel may reach another device: no remote copies, remote signals or barrier semaphores. Data moves between devices by JAX's collectives and lax.ppermute only.
A program may use at most 32 MiB of HBM per device.

```python
import math
import jax
import jax.numpy as jnp

D = 8192
NT = 8
HB = 2048


def level_of(own_key, extent, split, least, largest):
    gain = 1.0
    for axis_at, blocks in split:
        steps = jax.random.uniform(jax.random.fold_in(jax.random.fold_in(own_key, 6), axis_at), (blocks,), jnp.float32, least / len(split), largest / len(split))
        gain = gain * jnp.repeat(jnp.exp(steps), extent[axis_at] // blocks).reshape((-1,) + (1,) * (len(extent) - 1 - axis_at))
    return gain


def scatter_about(stream_key, dims, width, limit, shards=(), kind=jnp.bfloat16):
    array = width * jax.random.normal(stream_key, dims, jnp.float32)
    if shards:
        array = array * level_of(stream_key, dims, shards, -0.22, 0.18)
    return jnp.clip(array, -limit, limit).astype(kind)


def setup_inputs(seed: int = 0) -> dict:
    key_list = jax.random.split(jax.random.key(seed), 5)
    master = scatter_about(key_list[0], (D, NT, HB), 1.0, 6.0, ((0, 64), (2, 16)), jnp.float32)
    gradient = scatter_about(key_list[1], (D, NT, HB), 1.0, 6.0, ((0, 64), (2, 16)))
    first_moment = scatter_about(key_list[2], (D, NT, HB), 0.3, 3.0, ((0, 64), (2, 16)), jnp.float32)
    second_moment = jnp.clip(jnp.exp(math.log(4.0) - 3.6888794 * jax.random.uniform(key_list[3], (D, NT, HB), jnp.float32) ** level_of(key_list[3], (D, NT, HB), ((0, 64), (2, 16)), -0.2, 0.2)), 0.1, 4.0)
    return dict(master=master, gradient=gradient, first_moment=first_moment, second_moment=second_moment)


def reference(master, gradient, first_moment, second_moment):
    grad_full = gradient.astype(jnp.float32)
    moment_one = 0.9 * first_moment + 0.1 * grad_full
    moment_two = 0.95 * second_moment + 0.05 * grad_full * grad_full
    corr_one = 1.0 - 0.9 ** 10
    corr_two = 1.0 - 0.95 ** 10
    step_size = moment_one / corr_one / (jnp.sqrt(moment_two / corr_two) + 1e-08)
    new_master = master * (1.0 - 0.1 * 0.1) - 0.1 * step_size
    return (new_master, new_master.astype(jnp.bfloat16))
```

```python
import functools
import jax
import jax.numpy as jnp
from jax import lax
from jax.sharding import Mesh, PartitionSpec as P
from jax.experimental import pallas as pl
from jax.experimental.pallas import tpu as pltpu

NX, NH, LANES = 4, 4, 128


def adamw_update(master, gradient, first_moment, second_moment):
    grad_full = gradient.astype(jnp.float32)
    moment_one = 0.9 * first_moment + 0.1 * grad_full
    moment_two = 0.95 * second_moment + 0.05 * grad_full * grad_full
    corr_one = 1.0 - 0.9**10
    corr_two = 1.0 - 0.95**10
    step_size = moment_one / corr_one / (jnp.sqrt(moment_two / corr_two) + 1e-08)
    return master * (1.0 - 0.1 * 0.1) - 0.1 * step_size


def ring(axis, block, step):
    n = lax.axis_size(axis)
    return lax.ppermute(block, axis, [(i, (i + step) % n) for i in range(n)])


def onward(axis, fore, back):
    n, m = lax.axis_size(axis), lax.axis_size("tensor")
    pairs = [
        (i * m + t, (i + (1 if t % 2 == 0 else -1)) % n * m + t)
        for i in range(n)
        for t in range(m)
    ]
    core = lax.axis_index("tensor") % 2
    return lax.ppermute(jnp.where(core == 0, fore, back), (axis, "tensor"), pairs)


def around(axis, block):
    fore, back = ring(axis, block, 1), ring(axis, block, -1)
    fore, back = lax.optimization_barrier((fore, back))
    return [block, fore, back, onward(axis, fore, back)]


STEPS = (0, 1, -1, 2)


def place_kernel(parts, *refs):
    out = refs[-1]
    h = lax.axis_index("h")
    for ref, places in zip(refs[:-1], parts):
        for k, (dx, dh) in enumerate(places):
            col = lax.rem(h - dh + NH, NH) + NH * dx
            out[:, pl.ds(pl.multiple_of(col * LANES, LANES), LANES)] = ref[k]


def place(blocks, parts, rows, tile=256):
    return pl.pallas_call(
        functools.partial(place_kernel, parts),
        grid=(rows // tile,),
        out_shape=jax.ShapeDtypeStruct((rows, NX * NH * LANES), jnp.bfloat16),
        in_specs=[
            pl.BlockSpec((len(p), tile, LANES), lambda i: (0, i, 0)) for p in parts
        ],
        out_specs=pl.BlockSpec((tile, NX * NH * LANES), lambda i: (i, 0)),
        cost_estimate=pl.CostEstimate(
            flops=0, bytes_accessed=rows * NX * NH * LANES * 4, transcendentals=0
        ),
    )(*blocks)


def on_device(master, gradient, first_moment, second_moment):
    new_master = adamw_update(master, gradient, first_moment, second_moment)
    own = lax.all_to_all(
        new_master.astype(jnp.bfloat16), "tensor", split_axis=1, concat_axis=0, tiled=True
    )
    rows = own.shape[0]
    own = own.reshape(1, rows, LANES)
    own, up, down, far = around("h", own)
    blocks, parts = [], []
    for block, steps in (
        (own, (0,)),
        (jnp.concatenate([up, down]), (1, -1)),
        (far, (2,)),
    ):
        if blocks:
            block, blocks[-1] = lax.optimization_barrier((block, blocks[-1]))
        blocks.append(lax.all_gather(block, "x", axis=0, tiled=True))
        parts.append([(x, dh) for x in range(NX) for dh in steps])
    return (new_master, place(blocks, parts, rows)[:, None, :])


def solution(mesh):
    grid = mesh.devices
    fine = Mesh(
        grid.reshape(NX, NH, *grid.shape[1:]), ("x", "h", *mesh.axis_names[1:])
    )
    placed = P(("fsdp", "tensor"), None, ("x", "h"))
    return jax.shard_map(
        on_device,
        mesh=fine,
        in_specs=(placed,) * 4,
        out_specs=(placed, P("fsdp", "tensor", None)),
        check_vma=False,
    )
```

```python
import functools
import jax
import jax.numpy as jnp
from jax import lax
from jax.sharding import Mesh, PartitionSpec as P
from jax.experimental import pallas as pl
from jax.experimental.pallas import tpu as pltpu

NX, NH, LANES = 4, 4, 128


def adamw_update(master, gradient, first_moment, second_moment):
    grad_full = gradient.astype(jnp.float32)
    moment_one = 0.9 * first_moment + 0.1 * grad_full
    moment_two = 0.95 * second_moment + 0.05 * grad_full * grad_full
    corr_one = 1.0 - 0.9**10
    corr_two = 1.0 - 0.95**10
    step_size = moment_one / corr_one / (jnp.sqrt(moment_two / corr_two) + 1e-08)
    return master * (1.0 - 0.1 * 0.1) - 0.1 * step_size


def ring(axis, block, step):
    n = lax.axis_size(axis)
    return lax.ppermute(block, axis, [(i, (i + step) % n) for i in range(n)])


def onward(axis, fore, back):
    n, m = lax.axis_size(axis), lax.axis_size("tensor")
    pairs = [
        (i * m + t, (i + (1 if t % 2 == 0 else -1)) % n * m + t)
        for i in range(n)
        for t in range(m)
    ]
    core = lax.axis_index("tensor") % 2
    return lax.ppermute(jnp.where(core == 0, fore, back), (axis, "tensor"), pairs)


def place_kernel(parts, *refs):
    out = refs[-1]
    h = lax.axis_index("h")
    for ref, places in zip(refs[:-1], parts):
        for k, (dx, dh) in enumerate(places):
            col = lax.rem(h - dh + NH, NH) + NH * dx
            out[:, pl.ds(pl.multiple_of(col * LANES, LANES), LANES)] = ref[k]


def place(blocks, parts, rows, tile=256):
    return pl.pallas_call(
        functools.partial(place_kernel, parts),
        grid=(rows // tile,),
        out_shape=jax.ShapeDtypeStruct((rows, NX * NH * LANES), jnp.bfloat16),
        in_specs=[
            pl.BlockSpec((len(p), tile, LANES), lambda i: (0, i, 0)) for p in parts
        ],
        out_specs=pl.BlockSpec((tile, NX * NH * LANES), lambda i: (i, 0)),
        cost_estimate=pl.CostEstimate(
            flops=0, bytes_accessed=rows * NX * NH * LANES * 4, transcendentals=0
        ),
    )(*blocks)


def insert_kernel(col, block, base, out):
    del col, base
    out[...] = block[0]


def insert(rollout, block, dh):
    rows = block.shape[1]
    col = lax.rem(lax.axis_index("h") - dh + NH, NH).astype(jnp.int32)
    return pl.pallas_call(
        insert_kernel,
        grid_spec=pltpu.PrefetchScalarGridSpec(
            num_scalar_prefetch=1,
            grid=(NX, SPLIT),
            in_specs=[
                pl.BlockSpec((1, rows // SPLIT, LANES), lambda x, i, col: (x, i, 0)),
                pl.BlockSpec(memory_space=pl.ANY),
            ],
            out_specs=pl.BlockSpec(
                (rows // SPLIT, LANES), lambda x, i, col: (i, x * NH + col[0])
            ),
        ),
        out_shape=jax.ShapeDtypeStruct(rollout.shape, rollout.dtype),
        input_output_aliases={2: 0},
        cost_estimate=pl.CostEstimate(
            flops=0, bytes_accessed=4 * block.size, transcendentals=0
        ),
    )(col[None], block, rollout)


SPLIT = 1


def exchange(block):
    copies = jnp.broadcast_to(block[None], (NX, *block.shape))
    return lax.all_to_all(copies, "x", 0, 0).reshape(-1, *block.shape[1:])


def on_device(master, gradient, first_moment, second_moment):
    new_master = adamw_update(master, gradient, first_moment, second_moment)
    own = lax.all_to_all(
        new_master.astype(jnp.bfloat16), "tensor", split_axis=1, concat_axis=0, tiled=True
    )
    rows = own.shape[0]
    own = own.reshape(1, rows, LANES)
    halves = [
        lax.all_gather(part, "x", axis=0, tiled=True)
        for part in jnp.split(own, 2, axis=1)
    ]
    up, down = ring("h", own, 1), ring("h", own, -1)
    up, down, halves = lax.optimization_barrier((up, down, halves))
    far = onward("h", up, down)
    near = exchange(jnp.concatenate([up, down]))
    own = jnp.concatenate(halves, axis=1)
    parts = [
        [(x, 0) for x in range(NX)],
        [(x, dh) for x in range(NX) for dh in (1, -1)],
    ]
    rollout = place([own, near], parts, rows)
    far, near = lax.optimization_barrier((far, near))
    rollout = insert(rollout, exchange(far), 2)
    return (new_master, rollout[:, None, :])


def solution(mesh):
    grid = mesh.devices
    fine = Mesh(
        grid.reshape(NX, NH, *grid.shape[1:]), ("x", "h", *mesh.axis_names[1:])
    )
    placed = P(("fsdp", "tensor"), None, ("x", "h"))
    return jax.shard_map(
        on_device,
        mesh=fine,
        in_specs=(placed,) * 4,
        out_specs=(placed, P("fsdp", "tensor", None)),
        check_vma=False,
    )
```

```python
import functools
import jax
import jax.numpy as jnp
from jax import lax
from jax.sharding import Mesh, PartitionSpec as P
from jax.experimental import pallas as pl
from jax.experimental.pallas import tpu as pltpu

NX, NH, LANES = 4, 4, 128


def adamw_update(master, gradient, first_moment, second_moment):
    grad_full = gradient.astype(jnp.float32)
    moment_one = 0.9 * first_moment + 0.1 * grad_full
    moment_two = 0.95 * second_moment + 0.05 * grad_full * grad_full
    corr_one = 1.0 - 0.9**10
    corr_two = 1.0 - 0.95**10
    step_size = moment_one / corr_one / (jnp.sqrt(moment_two / corr_two) + 1e-08)
    return master * (1.0 - 0.1 * 0.1) - 0.1 * step_size


def swap_z(block, sign):
    n = lax.axis_size("tensor")
    pairs = [
        (h * n + t, (h + (sign if t % 2 == 0 else -sign)) % NH * n + t)
        for h in range(NH)
        for t in range(n)
    ]
    return lax.ppermute(block, ("h", "tensor"), pairs)


def place_kernel(parts, *refs):
    out = refs[-1]
    h = lax.axis_index("h")
    sign = 1 - 2 * lax.rem(lax.axis_index("tensor"), 2)
    for ref, steps in zip(refs[:-1], parts):
        for x in range(NX):
            for k, step in enumerate(steps):
                col = lax.rem(h - sign * step + NH, NH) + NH * x
                out[:, pl.ds(pl.multiple_of(col * LANES, LANES), LANES)] = ref[
                    x * len(steps) + k
                ]


def place(blocks, parts, rows, tile=256):
    return pl.pallas_call(
        functools.partial(place_kernel, parts),
        grid=(rows // tile,),
        out_shape=jax.ShapeDtypeStruct((rows, NX * NH * LANES), jnp.bfloat16),
        in_specs=[
            pl.BlockSpec((NX * len(p), tile, LANES), lambda i: (0, i, 0)) for p in parts
        ],
        out_specs=pl.BlockSpec((tile, NX * NH * LANES), lambda i: (i, 0)),
        compiler_params=pltpu.CompilerParams(vmem_limit_bytes=8 << 20),
        cost_estimate=pl.CostEstimate(
            flops=0, bytes_accessed=rows * NX * NH * LANES * 4, transcendentals=0
        ),
    )(*blocks)


def insert_kernel(block, base, out, sems):
    del base
    h = lax.rem(lax.axis_index("h") + 2, NH)
    copies = [
        pltpu.make_async_copy(
            block.at[x],
            out.at[:, pl.ds(pl.multiple_of((h + NH * x) * LANES, LANES), LANES)],
            sems.at[x],
        )
        for x in range(NX)
    ]
    for c in copies:
        c.start()
    for c in copies:
        c.wait()


def insert(rollout, block):
    return pl.pallas_call(
        insert_kernel,
        in_specs=[
            pl.BlockSpec(memory_space=pltpu.VMEM),
            pl.BlockSpec(memory_space=pl.ANY),
        ],
        out_specs=pl.BlockSpec(memory_space=pl.ANY),
        out_shape=jax.ShapeDtypeStruct(rollout.shape, rollout.dtype),
        scratch_shapes=[pltpu.SemaphoreType.DMA((NX,))],
        input_output_aliases={1: 0},
        compiler_params=pltpu.CompilerParams(vmem_limit_bytes=4 << 20),
        cost_estimate=pl.CostEstimate(
            flops=0, bytes_accessed=4 * block.size, transcendentals=0
        ),
    )(block, rollout)


def exchange(block):
    copies = jnp.broadcast_to(block[None], (NX, *block.shape))
    return lax.all_to_all(copies, "x", 0, 0).reshape(-1, *block.shape[1:])


def on_device(master, gradient, first_moment, second_moment):
    new_master = adamw_update(master, gradient, first_moment, second_moment)
    own = lax.all_to_all(
        new_master.astype(jnp.bfloat16), "tensor", split_axis=1, concat_axis=0, tiled=True
    )
    rows = own.shape[0]
    own = own.reshape(1, rows, LANES)
    one, other = swap_z(own, 1), swap_z(own, -1)
    halves = [
        lax.all_gather(part, "x", axis=0, tiled=True)
        for part in jnp.split(own, 2, axis=1)
    ]
    own = jnp.concatenate(halves, axis=1)
    one, own = lax.optimization_barrier((one, own))
    far = swap_z(one, 1)
    near = exchange(jnp.concatenate([one, other]))
    rollout = place([own, near], [(0,), (1, -1)], rows)
    far, near = lax.optimization_barrier((far, near))
    rollout = insert(rollout, exchange(far))
    return (new_master, rollout[:, None, :])


def solution(mesh):
    grid = mesh.devices
    fine = Mesh(
        grid.reshape(NX, NH, *grid.shape[1:]), ("x", "h", *mesh.axis_names[1:])
    )
    placed = P(("fsdp", "tensor"), None, ("x", "h"))
    return jax.shard_map(
        on_device,
        mesh=fine,
        in_specs=(placed,) * 4,
        out_specs=(placed, P("fsdp", "tensor", None)),
        check_vma=False,
    )
```

```python
import functools
import jax
import jax.numpy as jnp
from jax import lax
from jax.sharding import Mesh, PartitionSpec as P
from jax.experimental import pallas as pl
from jax.experimental.pallas import tpu as pltpu

NX, NH, LANES = 4, 4, 128


def adamw_update(master, gradient, first_moment, second_moment):
    grad_full = gradient.astype(jnp.float32)
    moment_one = 0.9 * first_moment + 0.1 * grad_full
    moment_two = 0.95 * second_moment + 0.05 * grad_full * grad_full
    corr_one = 1.0 - 0.9**10
    corr_two = 1.0 - 0.95**10
    step_size = moment_one / corr_one / (jnp.sqrt(moment_two / corr_two) + 1e-08)
    return master * (1.0 - 0.1 * 0.1) - 0.1 * step_size


def ring(axis, block, step):
    n = lax.axis_size(axis)
    return lax.ppermute(block, axis, [(i, (i + step) % n) for i in range(n)])


def onward(axis, fore, back):
    n, m = lax.axis_size(axis), lax.axis_size("tensor")
    pairs = [
        (i * m + t, (i + (1 if t % 2 == 0 else -1)) % n * m + t)
        for i in range(n)
        for t in range(m)
    ]
    core = lax.axis_index("tensor") % 2
    return lax.ppermute(jnp.where(core == 0, fore, back), (axis, "tensor"), pairs)


def place_kernel(parts, *refs):
    out = refs[-1]
    h = lax.axis_index("h")
    for ref, places in zip(refs[:-1], parts):
        for k, (dx, dh) in enumerate(places):
            col = lax.rem(h - dh + NH, NH) + NH * dx
            out[:, pl.ds(pl.multiple_of(col * LANES, LANES), LANES)] = ref[k]


def place(blocks, parts, rows, tile=256):
    return pl.pallas_call(
        functools.partial(place_kernel, parts),
        grid=(rows // tile,),
        out_shape=jax.ShapeDtypeStruct((rows, NX * NH * LANES), jnp.bfloat16),
        in_specs=[
            pl.BlockSpec((len(p), tile, LANES), lambda i: (0, i, 0)) for p in parts
        ],
        out_specs=pl.BlockSpec((tile, NX * NH * LANES), lambda i: (i, 0)),
        compiler_params=pltpu.CompilerParams(vmem_limit_bytes=8 << 20),
        cost_estimate=pl.CostEstimate(
            flops=0, bytes_accessed=rows * NX * NH * LANES * 4, transcendentals=0
        ),
    )(*blocks)


def insert_kernel(block, base, out, sems):
    del base
    h = lax.rem(lax.axis_index("h") + 2, NH)
    copies = [
        pltpu.make_async_copy(
            block.at[x],
            out.at[:, pl.ds(pl.multiple_of((h + NH * x) * LANES, LANES), LANES)],
            sems.at[x],
        )
        for x in range(NX)
    ]
    for c in copies:
        c.start()
    for c in copies:
        c.wait()


def insert(rollout, block):
    return pl.pallas_call(
        insert_kernel,
        in_specs=[
            pl.BlockSpec(memory_space=pltpu.VMEM),
            pl.BlockSpec(memory_space=pl.ANY),
        ],
        out_specs=pl.BlockSpec(memory_space=pl.ANY),
        out_shape=jax.ShapeDtypeStruct(rollout.shape, rollout.dtype),
        scratch_shapes=[pltpu.SemaphoreType.DMA((NX,))],
        input_output_aliases={1: 0},
        compiler_params=pltpu.CompilerParams(vmem_limit_bytes=4 << 20),
        cost_estimate=pl.CostEstimate(
            flops=0, bytes_accessed=4 * block.size, transcendentals=0
        ),
    )(block, rollout)


def exchange(block):
    copies = jnp.broadcast_to(block[None], (NX, *block.shape))
    return lax.all_to_all(copies, "x", 0, 0).reshape(-1, *block.shape[1:])


def on_device(master, gradient, first_moment, second_moment):
    new_master = adamw_update(master, gradient, first_moment, second_moment)
    own = lax.all_to_all(
        new_master.astype(jnp.bfloat16), "tensor", split_axis=1, concat_axis=0, tiled=True
    )
    rows = own.shape[0]
    own = own.reshape(1, rows, LANES)
    halves = [
        lax.all_gather(part, "x", axis=0, tiled=True)
        for part in jnp.split(own, 2, axis=1)
    ]
    up, down = ring("h", own, 1), ring("h", own, -1)
    up, down, halves = lax.optimization_barrier((up, down, halves))
    far = onward("h", up, down)
    near = exchange(jnp.concatenate([up, down]))
    own = jnp.concatenate(halves, axis=1)
    parts = [
        [(x, 0) for x in range(NX)],
        [(x, dh) for x in range(NX) for dh in (1, -1)],
    ]
    rollout = place([own, near], parts, rows)
    far, near = lax.optimization_barrier((far, near))
    rollout = insert(rollout, exchange(far))
    return (new_master, rollout[:, None, :])


def solution(mesh):
    grid = mesh.devices
    fine = Mesh(
        grid.reshape(NX, NH, *grid.shape[1:]), ("x", "h", *mesh.axis_names[1:])
    )
    placed = P(("fsdp", "tensor"), None, ("x", "h"))
    return jax.shard_map(
        on_device,
        mesh=fine,
        in_specs=(placed,) * 4,
        out_specs=(placed, P("fsdp", "tensor", None)),
        check_vma=False,
    )
```
